256 devices in a mesh: tp: 8 (over y, core), ex: 32 (over z, x).
Axes of the slice: x: 4, y: 4, z: 8, core: 2. Of those that a mesh axis runs over, the one named last changes fastest.
Arguments:
- token_ids: int32 [128, 128], P('ex'), may hold values from 0 to 128000, as said below
- attn_out: bfloat16 [128, 128, 4096], P('ex', None, 'tp'), may hold values from -6 to 6
- cotangent: bfloat16 [128, 128, 4096], P('ex', None, 'tp'), may hold values from -0.59765625 to 0.59765625
- basis_in: bfloat16 [4096, 4096], P('tp', 'ex'), may hold values from -0.09375 to 0.09375
- basis_out: bfloat16 [4096, 4096], P('tp', 'ex'), may hold values from -0.09375 to 0.09375
Outputs:
- corrections: float32 [4096, 4096], P('tp', 'ex')
The draws below stay inside these ranges and needn't reach their ends.
Inputs may be any that keep to these rules, and one draw needn't show every extreme that they name: `token_ids`: 0 marks padding, which fills every sequence after its last real token; position 0 of every sequence holds 128000.
All inputs are finite; a program needn't handle non-finite values.
Results may differ from the reference program's by a relative error of at most 0.00084.
Values may be sent and summed in bfloat16 or wider, within the bound.
A program may use at most 128 MiB of HBM per device.

```python
import jax
import jax.numpy as jnp
from jax import lax

D = 4096
LENGTH = 128
SEQUENCES = 128


def draw_token_ids(key, part):
    key = jax.random.fold_in(key, 11)
    key_len = jax.random.fold_in(key, 1)
    key_tok = jax.random.fold_in(key, 2)
    lengths = jax.random.randint(key_len, (SEQUENCES, 1), LENGTH // 2, LENGTH)
    token_draw = jax.random.randint(key_tok, (SEQUENCES, LENGTH), 1, 128001)
    position = jnp.arange(LENGTH, dtype=jnp.int32)[None, :]
    filled = jnp.where(position < lengths, token_draw, 0)
    return jnp.where(position == 0, 128000, filled).astype(jnp.int32)


def block_scale(stream_key, extent, cuts, low, top_value):
    def one(axis_at, shards_of):
        draws = jax.random.uniform(jax.random.fold_in(jax.random.fold_in(stream_key, 6), axis_at), (shards_of,), jnp.float32, low / len(cuts), top_value / len(cuts))
        return jnp.repeat(jnp.exp(draws), extent[axis_at] // shards_of).reshape((-1,) + (1,) * (len(extent) - axis_at - 1))

    level = one(*cuts[0])
    for cut in cuts[1:]:
        level = level * one(*cut)
    return level


def noise(rng, shape, scale, bound, pieces=(), held_as=jnp.bfloat16):
    values = scale * jax.random.normal(rng, shape, jnp.float32)
    if pieces:
        values = values * block_scale(rng, shape, pieces, -0.22, 0.18)
    return jnp.clip(values, -bound, bound).astype(held_as)


def setup_inputs(seed: int = 0) -> dict:
    key_of = jax.random.split(jax.random.key(seed), 6)
    return {
        "token_ids": draw_token_ids(jax.random.fold_in(key_of[5], 71), 0),
        "attn_out": noise(key_of[1], (SEQUENCES, LENGTH, D), 1.0, 6.0, ((0, 32), (2, 8))),
        "cotangent": noise(key_of[2], (SEQUENCES, LENGTH, D), 0.1, 0.59765625, ((0, 32), (2, 8))),
        "basis_in": noise(key_of[3], (D, D), D ** -0.5, 0.09375, ((0, 8), (1, 32))),
        "basis_out": noise(key_of[4], (D, D), D ** -0.5, 0.09375, ((0, 8), (1, 32))),
    }


def reference(token_ids, attn_out, cotangent, basis_in, basis_out):
    keep_mask = (token_ids != 0).astype(jnp.bfloat16)[:, :, None]
    masked = cotangent * keep_mask
    flat_in = attn_out.reshape(SEQUENCES * LENGTH, D)
    flat_out = masked.reshape(SEQUENCES * LENGTH, D)
    rotated_in = jnp.dot(flat_in, basis_in, preferred_element_type=jnp.float32).astype(jnp.bfloat16)
    rotated_out = jnp.dot(flat_out, basis_out, preferred_element_type=jnp.float32).astype(jnp.bfloat16)
    rotated_in = rotated_in.reshape(SEQUENCES, LENGTH, D)
    rotated_out = rotated_out.reshape(SEQUENCES, LENGTH, D)

    def accumulate(running, pair_rows):
        left_rows, right_rows = pair_rows
        product = jnp.dot(left_rows.T, right_rows, preferred_element_type=jnp.float32)
        return running + product * product, None

    running = lax.scan(accumulate, jnp.zeros((D, D), jnp.float32), (rotated_in, rotated_out))[0]
    return running / SEQUENCES
```

```python
import functools

import jax
import jax.numpy as jnp
from jax import lax
from jax.experimental import pallas as pl
from jax.experimental.pallas import tpu as pltpu
from jax.sharding import PartitionSpec as P

MESH = pl.DeviceIdType.MESH
BF16 = jnp.bfloat16
F32 = jnp.float32
STEP = {(0, 0): 0, (0, 1): 1, (3, 0): 2, (1, 1): 3, (3, 1): 4, (1, 0): 5, (2, 0): 6, (2, 1): 7}


def remote(src, dst, send, recv, device):
    return pltpu.make_async_remote_copy(
        src_ref=src, dst_ref=dst, send_sem=send, recv_sem=recv, device_id=device, device_id_type=MESH
    )


def dot(a, b):
    return jnp.dot(a, b, preferred_element_type=F32)


def kernel(
    attn, cot, b_in, b_out, out,
    a, b, s1, relay, s2, fin, rq, acc, osend, orecv,
    local_sem, swap_send, swap_recv, b_send, b_recv, a_send, a_recv,
    s1_send, s1_recv, s2_send, s2_recv, r_send, r_recv, q_send, q_recv, o_send, o_recv,
):
    t, e = lax.axis_index("tp"), lax.axis_index("ex")
    y, c = lax.div(t, 2), lax.rem(t, 2)
    z, x = lax.div(e, 4), lax.rem(e, 4)
    xr, xl = (t, z * 4 + lax.rem(x + 1, 4)), (t, z * 4 + lax.rem(x + 3, 4))
    yr, yl = (lax.rem(y + 1, 4) * 2 + c, e), (lax.rem(y + 3, 4) * 2 + c, e)
    zr, zl = (t, lax.rem(z + 1, 8) * 4 + x), (t, lax.rem(z + 7, 8) * 4 + x)
    partner = (y * 2 + 1 - c, e)
    rr = (xr[0] * (1 - c) + yr[0] * c, xr[1] * (1 - c) + yr[1] * c)
    rl = (xl[0] * (1 - c) + yl[0] * c, xl[1] * (1 - c) + yl[1] * c)

    barrier = pltpu.get_barrier_semaphore()
    for device in (xr, xl, yr, yl, zr, zl, partner):
        pl.semaphore_signal(barrier, inc=1, device_id=device, device_id_type=MESH)
    pl.semaphore_wait(barrier, 7)

    half = pl.ds(pl.multiple_of(c * 512, 512), 512)
    other = pl.ds(pl.multiple_of((1 - c) * 512, 512), 512)

    def b_cols(zz):
        zz = lax.rem(zz + 16, 8)
        return lax.div(zz, 2), pl.ds(pl.multiple_of(lax.rem(zz, 2) * 128, 128), 128)

    own_pair, own_lanes = b_cols(z)

    def swap(mine_a, mine_b, theirs_a, theirs_b):
        def copies():
            yield pltpu.make_async_copy(mine_b, b.at[own_pair, half, own_lanes], local_sem.at[2])
            yield remote(theirs_b, b.at[own_pair, half, own_lanes], swap_send.at[2], swap_recv.at[2], partner)
            for u in range(2):
                yield pltpu.make_async_copy(mine_a.at[u], a.at[u, :, half], local_sem.at[u])
                yield remote(theirs_a.at[u], a.at[u, :, half], swap_send.at[u], swap_recv.at[u], partner)

        return copies

    @pl.when(c == 0)
    def _():
        for copy in swap(attn, b_in, cot, b_out)():
            copy.start()

    @pl.when(c == 1)
    def _():
        for copy in swap(cot, b_out, attn, b_in)():
            copy.start()

    def swapped_b():
        pltpu.make_async_copy(b_in, b.at[own_pair, half, own_lanes], local_sem.at[2]).wait()
        remote(b_in, b.at[own_pair, other, own_lanes], swap_send.at[2], swap_recv.at[2], partner).wait()

    def swapped_a(u):
        pltpu.make_async_copy(attn.at[u], a.at[u, :, half], local_sem.at[u]).wait()
        remote(attn.at[u], a.at[u, :, other], swap_send.at[u], swap_recv.at[u], partner).wait()

    def b_copy(hop, way, receive=False):
        origin = z - hop if way == 0 else z + hop
        if receive:
            origin = origin - 1 if way == 0 else origin + 1
        pair, lanes = b_cols(origin)
        rows = pl.ds(0, 1024) if hop < 3 else pl.ds(512 * way, 512)
        block = b.at[pair, rows, lanes]
        return remote(block, block, b_send.at[hop, way], b_recv.at[hop, way], zr if way == 0 else zl)

    a_moves = [(0, 2, 0), (1, 3, 1), (1, 4, 0), (0, 5, 1), (2, 6, 0), (3, 7, 1)]

    def a_copy(move):
        src, dst, way = a_moves[move]
        return remote(a.at[src], a.at[dst], a_send.at[move], a_recv.at[dst], xr if way == 0 else xl)

    swapped_b()
    for way in range(2):
        b_copy(0, way).start()
    swapped_a(0)
    a_copy(0).start()
    swapped_a(1)
    a_copy(1).start()
    a_copy(2).start()
    a_copy(3).start()
    for hop in range(4):
        for way in range(2):
            b_copy(hop, way, receive=True).wait_recv()
            if hop < 3:
                b_copy(hop + 1, way).start()
        if hop == 1:
            for move in range(2):
                a_copy(move).wait_recv()
                a_copy(move + 4).start()

    y_right, y_left, y_across = lax.rem(y + 1, 4), lax.rem(y + 3, 4), lax.rem(y + 2, 4)

    def relay_copy(k, way):
        return remote(s1.at[k, way], relay.at[k, way], s1_send.at[k, way], s1_recv.at[k, way], yr if way == 0 else yl)

    def fin_copy(k, way):
        return remote(s2.at[k, way], fin.at[k, way], s2_send.at[k, way], s2_recv.at[k, way], yr if way == 0 else yl)

    def r_copy(k, move):
        src, dst, way = [
            (rq.at[c, 0, k], rq.at[c, 3, k], 0),
            (rq.at[c, 0, k], rq.at[c, 1, k], 1),
            (rq.at[c, 3, k, pl.ds(0, 128)], rq.at[c, 2, k, pl.ds(0, 128)], 0),
            (rq.at[c, 1, k, pl.ds(128, 128)], rq.at[c, 2, k, pl.ds(128, 128)], 1),
        ][move]
        return remote(src, dst, r_send.at[k, move], r_recv.at[k, move], rr if way == 0 else rl)

    def q_copy(k, slot, receive=False):
        block = rq.at[1 - c if receive else c, slot, k]
        return remote(block, block, q_send.at[k, slot], q_recv.at[k, slot], partner)

    def tick(i, carry):
        def stage(lag, body):
            k = i - lag
            pl.when((k >= 0) & (k < 8))(functools.partial(body, k))

        def first(k):
            @pl.when(k >= 4)
            def _():
                remote(a.at[k], a.at[k], a_send.at[0], a_recv.at[k], xr).wait_recv()

            p = dot(a[k], b[y_across]).astype(BF16)
            s1[k, 0] = p[:128]
            s1[k, 1] = p[128:]
            for way in range(2):
                relay_copy(k, way).start()

        def second(k):
            for way, target in ((0, y_right), (1, y_left)):
                p = dot(a[k], b[target])
                relay_copy(k, way).wait_recv()
                if way == 0:
                    s2[k, 0, :128] = (p[:128] + relay[k, 0].astype(F32)).astype(BF16)
                    s2[k, 0, 128:] = p[128:].astype(BF16)
                else:
                    s2[k, 1, :128] = p[:128].astype(BF16)
                    s2[k, 1, 128:] = (p[128:] + relay[k, 1].astype(F32)).astype(BF16)
                fin_copy(k, way).start()

        def third(k):
            p = dot(a[k], b[y])
            for way in range(2):
                fin_copy(k, way).wait_recv()
            rq[c, 0, k] = (p + fin[k, 0].astype(F32) + fin[k, 1].astype(F32)).astype(BF16)
            r_copy(k, 0).start()
            r_copy(k, 1).start()
            q_copy(k, 0).start()

        def fourth(k):
            for move, slot in ((0, 3), (1, 1)):
                r_copy(k, move).wait_recv()
                r_copy(k, move + 2).start()
                q_copy(k, slot).start()

        def fifth(k):
            r_copy(k, 2).wait_recv()
            r_copy(k, 3).wait_recv()
            q_copy(k, 2).start()

        stage(0, first)
        stage(1, second)
        stage(2, third)
        stage(3, fourth)
        stage(4, fifth)
        return carry

    lax.fori_loop(0, 12, tick, 0)

    lanes = pl.ds(pl.multiple_of(c * 128, 128), 128)

    def take(k, carry):
        for slot in range(4):
            q_copy(k, slot, receive=True).wait_recv()
        return carry

    lax.fori_loop(0, 8, take, 0)
    acc[...] = jnp.zeros_like(acc)
    for ds in range(4):
        for u in range(2):

            def example(h, carry, ds=ds, u=u):
                rows = pl.ds(pl.multiple_of(h * 128, 128), 128)
                left = jnp.concatenate(
                    [rq[0, dx, STEP[(ds - dx) % 4, u], rows, lanes] for dx in range(4)], axis=1
                )
                for dy in range(4):
                    right = rq[1, dy, STEP[ds, u], rows, :]
                    coeff = lax.dot_general(left, right, (((0,), (0,)), ((), ())), preferred_element_type=F32)
                    acc[dy] += coeff * coeff
                return carry

            lax.fori_loop(0, 2, example, 0)

    def part(d, upper):
        zz = lax.rem(z + d + 16, 8)
        slot = lax.rem(lax.div(zz, 2) - y + 4, 4)
        return acc[slot, 256 * upper : 256 * upper + 256, pl.ds(pl.multiple_of(lax.rem(zz, 2) * 128, 128), 128)]

    def o_copy(way, i):
        return remote(osend.at[way, i], orecv.at[way, i], o_send.at[way, i], o_recv.at[way, i], zr if way == 0 else zl)

    for i in range(7):
        for way in range(2):
            d = 4 - (i + 1) // 2
            block = part(d if way == 0 else -d, (i % 2) ^ way)
            if i >= 2:
                o_copy(way, i - 2).wait_recv()
                block = block + orecv[way, i - 2]
            osend[way, i] = block
            o_copy(way, i).start()
    for i in (5, 6):
        for way in range(2):
            o_copy(way, i).wait_recv()
    for upper in range(2):
        total = (part(0, upper) + orecv[0, 6 - upper] + orecv[1, 5 + upper]) * (1.0 / 128.0)
        for s in range(2):
            place = lax.rem(x + 2 * upper + s, 4)
            out[pl.ds(pl.multiple_of(place * 128, 128), 128), :] = total[128 * s : 128 * s + 128]

    for hop in range(4):
        for way in range(2):
            b_copy(hop, way).wait_send()
    for move in range(6):
        a_copy(move).wait_send()

    def sent(k, carry):
        for way in range(2):
            relay_copy(k, way).wait_send()
            fin_copy(k, way).wait_send()
        for move in range(4):
            r_copy(k, move).wait_send()
            q_copy(k, move).wait_send()
        return carry

    lax.fori_loop(0, 8, sent, 0)
    for i in range(7):
        for way in range(2):
            o_copy(way, i).wait_send()


def on_device(token_ids, attn_out, cotangent, basis_in, basis_out):
    keep_mask = (token_ids != 0).astype(BF16)[:, :, None]
    masked = (cotangent * keep_mask).reshape(2, 256, 512)
    dma = pltpu.SemaphoreType.DMA
    return pl.pallas_call(
        kernel,
        out_shape=jax.ShapeDtypeStruct((512, 128), F32),
        in_specs=[pl.BlockSpec(memory_space=pl.ANY)] * 4,
        out_specs=pl.BlockSpec(memory_space=pltpu.VMEM),
        scratch_shapes=[
            pltpu.VMEM((8, 256, 1024), BF16),
            pltpu.VMEM((4, 1024, 256), BF16),
            pltpu.VMEM((8, 2, 128, 256), BF16),
            pltpu.VMEM((8, 2, 128, 256), BF16),
            pltpu.VMEM((8, 2, 256, 256), BF16),
            pltpu.VMEM((8, 2, 256, 256), BF16),
            pltpu.VMEM((2, 4, 8, 256, 256), BF16),
            pltpu.VMEM((4, 512, 256), F32),
            pltpu.VMEM((2, 7, 256, 128), F32),
            pltpu.VMEM((2, 7, 256, 128), F32),
            dma((3,)), dma((3,)), dma((3,)),
            dma((4, 2)), dma((4, 2)),
            dma((6,)), dma((8,)),
            dma((8, 2)), dma((8, 2)), dma((8, 2)), dma((8, 2)),
            dma((8, 4)), dma((8, 4)), dma((8, 4)), dma((8, 4)),
            dma((2, 7)), dma((2, 7)),
        ],
        compiler_params=pltpu.CompilerParams(
            collective_id=0, has_side_effects=True, vmem_limit_bytes=48 * 1024 * 1024
        ),
    )(attn_out.reshape(2, 256, 512), masked, basis_in, basis_out)


def solution(mesh):
    return jax.shard_map(
        on_device,
        mesh=mesh,
        in_specs=(
            P("ex", None),
            P("ex", None, "tp"),
            P("ex", None, "tp"),
            P("tp", "ex"),
            P("tp", "ex"),
        ),
        out_specs=P("tp", "ex"),
        check_vma=False,
    )
```

```python
import functools

import jax
import jax.numpy as jnp
from jax import lax
from jax.experimental import pallas as pl
from jax.experimental.pallas import tpu as pltpu
from jax.sharding import PartitionSpec as P

MESH = pl.DeviceIdType.MESH
BF16 = jnp.bfloat16
F32 = jnp.float32
STEP = {(0, 0): 0, (0, 1): 1, (3, 0): 2, (1, 1): 3, (3, 1): 4, (1, 0): 5, (2, 0): 6, (2, 1): 7}
LAG = 2


def remote(src, dst, send, recv, device):
    return pltpu.make_async_remote_copy(
        src_ref=src, dst_ref=dst, send_sem=send, recv_sem=recv, device_id=device, device_id_type=MESH
    )


def dot(a, b):
    return jnp.dot(a, b, preferred_element_type=F32)


def kernel(
    tokens, attn, cot, b_in, b_out, out,
    a, b, s1, relay, s2, fin, rq, acc, osend, orecv,
    local_sem, swap_send, swap_recv, b_send, b_recv, a_send, a_recv,
    s1_send, s1_recv, s2_send, s2_recv, r_send, r_recv, q_send, q_recv, o_send, o_recv,
):
    t, e = lax.axis_index("tp"), lax.axis_index("ex")
    y, c = lax.div(t, 2), lax.rem(t, 2)
    z, x = lax.div(e, 4), lax.rem(e, 4)
    xr, xl = (t, z * 4 + lax.rem(x + 1, 4)), (t, z * 4 + lax.rem(x + 3, 4))
    yr, yl = (lax.rem(y + 1, 4) * 2 + c, e), (lax.rem(y + 3, 4) * 2 + c, e)
    zr, zl = (t, lax.rem(z + 1, 8) * 4 + x), (t, lax.rem(z + 7, 8) * 4 + x)
    partner = (y * 2 + 1 - c, e)
    rr = (xr[0] * (1 - c) + yr[0] * c, xr[1] * (1 - c) + yr[1] * c)
    rl = (xl[0] * (1 - c) + yl[0] * c, xl[1] * (1 - c) + yl[1] * c)

    barrier = pltpu.get_barrier_semaphore()
    for device in (xr, xl, yr, yl, zr, zl, partner):
        pl.semaphore_signal(barrier, inc=1, device_id=device, device_id_type=MESH)
    pl.semaphore_wait(barrier, 7)

    half = pl.ds(pl.multiple_of(c * 512, 512), 512)
    other = pl.ds(pl.multiple_of((1 - c) * 512, 512), 512)

    def b_cols(zz):
        zz = lax.rem(zz + 16, 8)
        return lax.div(zz, 2), pl.ds(pl.multiple_of(lax.rem(zz, 2) * 128, 128), 128)

    own_pair, own_lanes = b_cols(z)

    def swap(mine_a, mine_b, theirs_a, theirs_b):
        def copies():
            yield pltpu.make_async_copy(mine_b, b.at[own_pair, half, own_lanes], local_sem.at[2])
            yield remote(theirs_b, b.at[own_pair, half, own_lanes], swap_send.at[2], swap_recv.at[2], partner)
            for u in range(2):
                yield pltpu.make_async_copy(mine_a.at[u], a.at[u, :, half], local_sem.at[u])
                yield remote(theirs_a.at[u], a.at[u, :, half], swap_send.at[u], swap_recv.at[u], partner)

        return copies

    @pl.when(c == 0)
    def _():
        for copy in swap(attn, b_in, cot, b_out)():
            copy.start()

    @pl.when(c == 1)
    def _():
        for copy in swap(cot, b_out, attn, b_in)():
            copy.start()

    def swapped_b():
        pltpu.make_async_copy(b_in, b.at[own_pair, half, own_lanes], local_sem.at[2]).wait()
        remote(b_in, b.at[own_pair, other, own_lanes], swap_send.at[2], swap_recv.at[2], partner).wait()

    def swapped_a(u):
        pltpu.make_async_copy(attn.at[u], a.at[u, :, half], local_sem.at[u]).wait()
        remote(attn.at[u], a.at[u, :, other], swap_send.at[u], swap_recv.at[u], partner).wait()

    def b_copy(hop, way, receive=False):
        origin = z - hop if way == 0 else z + hop
        if receive:
            origin = origin - 1 if way == 0 else origin + 1
        pair, lanes = b_cols(origin)
        rows = pl.ds(0, 1024) if hop < 3 else pl.ds(512 * way, 512)
        block = b.at[pair, rows, lanes]
        return remote(block, block, b_send.at[hop, way], b_recv.at[hop, way], zr if way == 0 else zl)

    a_moves = [(0, 2, 0), (1, 3, 1), (1, 4, 0), (0, 5, 1), (2, 6, 0), (3, 7, 1)]

    def a_copy(move):
        src, dst, way = a_moves[move]
        return remote(a.at[src], a.at[dst], a_send.at[move], a_recv.at[dst], xr if way == 0 else xl)

    def take_a(u):
        swapped_a(u)

        @pl.when(c == 1)
        def _():
            square = (128, 128)
            diagonal = lax.broadcasted_iota(jnp.int32, square, 0) == lax.broadcasted_iota(jnp.int32, square, 1)
            for h in range(2):
                keep = jnp.where(tokens[2 * u + h : 2 * u + h + 1, :] != 0, 1.0, 0.0).astype(F32)
                column = jnp.sum(jnp.where(diagonal, keep, 0.0), axis=1, keepdims=True).astype(BF16)
                a[u, 128 * h : 128 * h + 128, :] = a[u, 128 * h : 128 * h + 128, :] * column

    swapped_b()
    for way in range(2):
        b_copy(0, way).start()
    take_a(0)
    a_copy(0).start()
    take_a(1)
    a_copy(1).start()
    a_copy(2).start()
    a_copy(3).start()
    acc[...] = jnp.zeros_like(acc)
    for hop in range(4):
        for way in range(2):
            b_copy(hop, way, receive=True).wait_recv()
            if hop < 3:
                b_copy(hop + 1, way).start()
        if hop == 1:
            for move in range(2):
                a_copy(move).wait_recv()
                a_copy(move + 4).start()

    y_right, y_left, y_across = lax.rem(y + 1, 4), lax.rem(y + 3, 4), lax.rem(y + 2, 4)

    def relay_copy(k, way):
        return remote(s1.at[k, way], relay.at[k, way], s1_send.at[k, way], s1_recv.at[k, way], yr if way == 0 else yl)

    def fin_copy(k, way):
        return remote(s2.at[k, way], fin.at[k, way], s2_send.at[k, way], s2_recv.at[k, way], yr if way == 0 else yl)

    def r_copy(k, move):
        src, dst, way = [
            (rq.at[c, 0, k], rq.at[c, 3, k], 0),
            (rq.at[c, 0, k], rq.at[c, 1, k], 1),
            (rq.at[c, 3, k, pl.ds(0, 128)], rq.at[c, 2, k, pl.ds(0, 128)], 0),
            (rq.at[c, 1, k, pl.ds(128, 128)], rq.at[c, 2, k, pl.ds(128, 128)], 1),
        ][move]
        return remote(src, dst, r_send.at[k, move], r_recv.at[k, move], rr if way == 0 else rl)

    def q_copy(k, slot, receive=False):
        block = rq.at[1 - c if receive else c, slot, k]
        return remote(block, block, q_send.at[k, slot], q_recv.at[k, slot], partner)

    def q_copy_in(k, slot):
        block = rq.at[0, slot, k, pl.ds(128, 128)]
        return remote(block, block, q_send.at[k, slot], q_recv.at[k, slot], partner)

    def hand_over(k, slot, act):
        pl.when(c == 0)(lambda: getattr(q_copy_in(k, slot), act)())
        pl.when(c == 1)(lambda: getattr(q_copy(k, slot), act)())

    def tick(i, carry):
        def stage(lag, body):
            k = i - lag * LAG
            pl.when((k >= 0) & (k < 8))(functools.partial(body, k))

        def first(k):
            @pl.when(k >= 4)
            def _():
                remote(a.at[k], a.at[k], a_send.at[0], a_recv.at[k], xr).wait_recv()

            p = dot(a[k], b[y_across]).astype(BF16)
            s1[k, 0] = p[:128]
            s1[k, 1] = p[128:]
            for way in range(2):
                relay_copy(k, way).start()

        def second(k):
            for way, target in ((0, y_right), (1, y_left)):
                p = dot(a[k], b[target])
                relay_copy(k, way).wait_recv()
                if way == 0:
                    s2[k, 0, :128] = (p[:128] + relay[k, 0].astype(F32)).astype(BF16)
                    s2[k, 0, 128:] = p[128:].astype(BF16)
                else:
                    s2[k, 1, :128] = p[:128].astype(BF16)
                    s2[k, 1, 128:] = (p[128:] + relay[k, 1].astype(F32)).astype(BF16)
                fin_copy(k, way).start()

        def third(k):
            p = dot(a[k], b[y])
            for way in range(2):
                fin_copy(k, way).wait_recv()
            total = p + fin[k, 0].astype(F32) + fin[k, 1].astype(F32)

            @pl.when(c == 0)
            def _():
                rq[0, 0, k] = total.T.astype(BF16)

            @pl.when(c == 1)
            def _():
                rq[1, 0, k] = total.astype(BF16)

            r_copy(k, 0).start()
            r_copy(k, 1).start()
            hand_over(k, 0, "start")

        def fourth(k):
            for move, slot in ((0, 3), (1, 1)):
                r_copy(k, move).wait_recv()
                r_copy(k, move + 2).start()
                hand_over(k, slot, "start")

        def fifth(k):
            r_copy(k, 2).wait_recv()
            r_copy(k, 3).wait_recv()
            hand_over(k, 2, "start")

        stage(0, first)
        stage(1, second)
        stage(2, third)
        stage(3, fourth)
        stage(4, fifth)
        return carry

    lax.fori_loop(0, 8 + 4 * LAG, tick, 0)

    odd = lax.rem(z, 2)

    lanes = pl.ds(pl.multiple_of(c * 128, 128), 128)

    def product(pair):
        slot = lax.rem(pair - y + 4, 4)

        @pl.when(c == 0)
        def _():
            def take(k, carry):
                q_copy(k, slot, receive=True).wait_recv()
                return carry

            lax.fori_loop(0, 8, take, 0)

        for ds in range(4):
            for u in range(2):
                squares = 0.0
                for h in range(2):
                    rows = slice(128 * h, 128 * h + 128)
                    left = jnp.concatenate(
                        [rq[0, dx, STEP[(ds - dx) % 4, u], lanes, rows] for dx in range(4)], axis=0
                    )
                    coeff = dot(left, rq[1, slot, STEP[ds, u], rows, :])
                    squares = squares + coeff * coeff
                acc[pair] += squares

    def part(d, upper):
        zz = lax.rem(z + d + 16, 8)
        return acc[lax.div(zz, 2), 256 * upper : 256 * upper + 256, pl.ds(pl.multiple_of(lax.rem(zz, 2) * 128, 128), 128)]

    def o_copy(way, i):
        return remote(osend.at[way, i], orecv.at[way, i], o_send.at[way, i], o_recv.at[way, i], zr if way == 0 else zl)

    def pass_on(way, i):
        d = 4 - (i + 1) // 2
        block = part(d if way == 0 else -d, (i % 2) ^ way)
        if i >= 2:
            o_copy(way, i - 2).wait_recv()
            block = block + orecv[way, i - 2]
        osend[way, i] = block
        o_copy(way, i).start()

    even = odd == 0

    def passes(steps_even, steps_odd):
        for now, steps in ((even, steps_even), (jnp.logical_not(even), steps_odd)):

            @pl.when(now)
            def _(steps=steps):
                for way, i in steps:
                    pass_on(way, i)

    @pl.when(c == 1)
    def _():
        def take(k, carry):
            for slot in range(4):
                q_copy_in(k, slot).wait_recv()
            return carry

        lax.fori_loop(0, 8, take, 0)

    late = [(way, i) for i in range(3, 7) for way in range(2)]
    steps = [
        ([(0, 0), (1, 0), (1, 1)], [(0, 0), (1, 0), (0, 1)]),
        ([(0, 1), (0, 2), (1, 2)], [(1, 1), (0, 2), (1, 2)]),
    ]
    def squares_of(n, carry):
        offset = jnp.where(n == 0, 2, jnp.where(n == 1, 1 + 2 * odd, jnp.where(n == 2, 3 - 2 * odd, 0)))
        product(lax.rem(lax.div(z, 2) + offset, 4))
        for m in range(2):
            pl.when(n == m)(functools.partial(passes, *steps[m]))
        return carry

    lax.fori_loop(0, 4, squares_of, 0)
    for way, i in late:
        pass_on(way, i)

    for i in (5, 6):
        for way in range(2):
            o_copy(way, i).wait_recv()
    for upper in range(2):
        total = (part(0, upper) + orecv[0, 6 - upper] + orecv[1, 5 + upper]) * (1.0 / 128.0)
        for s in range(2):
            place = lax.rem(x + 2 * upper + s, 4)
            out[pl.ds(pl.multiple_of(place * 128, 128), 128), :] = total[128 * s : 128 * s + 128]

    for hop in range(4):
        for way in range(2):
            b_copy(hop, way).wait_send()
    for move in range(6):
        a_copy(move).wait_send()

    def sent(k, carry):
        for way in range(2):
            relay_copy(k, way).wait_send()
            fin_copy(k, way).wait_send()
        for move in range(4):
            r_copy(k, move).wait_send()
            hand_over(k, move, "wait_send")
        return carry

    lax.fori_loop(0, 8, sent, 0)
    for i in range(7):
        for way in range(2):
            o_copy(way, i).wait_send()


def on_device(token_ids, attn_out, cotangent, basis_in, basis_out):
    dma = pltpu.SemaphoreType.DMA
    return pl.pallas_call(
        kernel,
        out_shape=jax.ShapeDtypeStruct((512, 128), F32),
        in_specs=[pl.BlockSpec(memory_space=pltpu.VMEM)] + [pl.BlockSpec(memory_space=pl.ANY)] * 4,
        out_specs=pl.BlockSpec(memory_space=pltpu.VMEM),
        scratch_shapes=[
            pltpu.VMEM((8, 256, 1024), BF16),
            pltpu.VMEM((4, 1024, 256), BF16),
            pltpu.VMEM((8, 2, 128, 256), BF16),
            pltpu.VMEM((8, 2, 128, 256), BF16),
            pltpu.VMEM((8, 2, 256, 256), BF16),
            pltpu.VMEM((8, 2, 256, 256), BF16),
            pltpu.VMEM((2, 4, 8, 256, 256), BF16),
            pltpu.VMEM((4, 512, 256), F32),
            pltpu.VMEM((2, 7, 256, 128), F32),
            pltpu.VMEM((2, 7, 256, 128), F32),
            dma((3,)), dma((3,)), dma((3,)),
            dma((4, 2)), dma((4, 2)),
            dma((6,)), dma((8,)),
            dma((8, 2)), dma((8, 2)), dma((8, 2)), dma((8, 2)),
            dma((8, 4)), dma((8, 4)), dma((8, 4)), dma((8, 4)),
            dma((2, 7)), dma((2, 7)),
        ],
        compiler_params=pltpu.CompilerParams(
            collective_id=0, has_side_effects=True, vmem_limit_bytes=48 * 1024 * 1024
        ),
    )(token_ids, attn_out.reshape(2, 256, 512), cotangent.reshape(2, 256, 512), basis_in, basis_out)


def solution(mesh):
    return jax.shard_map(
        on_device,
        mesh=mesh,
        in_specs=(
            P("ex", None),
            P("ex", None, "tp"),
            P("ex", None, "tp"),
            P("tp", "ex"),
            P("tp", "ex"),
        ),
        out_specs=P("tp", "ex"),
        check_vma=False,
    )
```

```python
import functools

import jax
import jax.numpy as jnp
from jax import lax
from jax.experimental import pallas as pl
from jax.experimental.pallas import tpu as pltpu
from jax.sharding import PartitionSpec as P

MESH = pl.DeviceIdType.MESH
BF16 = jnp.bfloat16
F32 = jnp.float32
STEP = {(0, 0): 0, (0, 1): 1, (3, 0): 2, (1, 1): 3, (3, 1): 4, (1, 0): 5, (2, 0): 6, (2, 1): 7}
LAG = 2


def remote(src, dst, send, recv, device):
    return pltpu.make_async_remote_copy(
        src_ref=src, dst_ref=dst, send_sem=send, recv_sem=recv, device_id=device, device_id_type=MESH
    )


def dot(a, b):
    return jnp.dot(a, b, preferred_element_type=F32)


def kernel(
    tokens, attn, cot, b_in, b_out, out,
    a, b, s1, relay, s2, fin, rq, acc, osend, orecv,
    local_sem, swap_send, swap_recv, b_send, b_recv, a_send, a_recv,
    s1_send, s1_recv, s2_send, s2_recv, r_send, r_recv, q_send, q_recv, o_send, o_recv,
):
    t, e = lax.axis_index("tp"), lax.axis_index("ex")
    y, c = lax.div(t, 2), lax.rem(t, 2)
    z, x = lax.div(e, 4), lax.rem(e, 4)
    xr, xl = (t, z * 4 + lax.rem(x + 1, 4)), (t, z * 4 + lax.rem(x + 3, 4))
    yr, yl = (lax.rem(y + 1, 4) * 2 + c, e), (lax.rem(y + 3, 4) * 2 + c, e)
    zr, zl = (t, lax.rem(z + 1, 8) * 4 + x), (t, lax.rem(z + 7, 8) * 4 + x)
    partner = (y * 2 + 1 - c, e)
    rr = (xr[0] * (1 - c) + yr[0] * c, xr[1] * (1 - c) + yr[1] * c)
    rl = (xl[0] * (1 - c) + yl[0] * c, xl[1] * (1 - c) + yl[1] * c)

    barrier = pltpu.get_barrier_semaphore()
    for device in (xr, xl, yr, yl, zr, zl, partner):
        pl.semaphore_signal(barrier, inc=1, device_id=device, device_id_type=MESH)
    pl.semaphore_wait(barrier, 7)

    half = pl.ds(pl.multiple_of(c * 512, 512), 512)
    other = pl.ds(pl.multiple_of((1 - c) * 512, 512), 512)

    def b_cols(zz):
        zz = lax.rem(zz + 16, 8)
        return lax.div(zz, 2), pl.ds(pl.multiple_of(lax.rem(zz, 2) * 128, 128), 128)

    own_pair, own_lanes = b_cols(z)

    def swap(mine_a, mine_b, theirs_a, theirs_b):
        def copies():
            yield pltpu.make_async_copy(mine_b, b.at[own_pair, half, own_lanes], local_sem.at[2])
            yield remote(theirs_b, b.at[own_pair, half, own_lanes], swap_send.at[2], swap_recv.at[2], partner)
            for u in range(2):
                yield pltpu.make_async_copy(mine_a.at[u], a.at[u, :, half], local_sem.at[u])
                yield remote(theirs_a.at[u], a.at[u, :, half], swap_send.at[u], swap_recv.at[u], partner)

        return copies

    @pl.when(c == 0)
    def _():
        for copy in swap(attn, b_in, cot, b_out)():
            copy.start()

    @pl.when(c == 1)
    def _():
        for copy in swap(cot, b_out, attn, b_in)():
            copy.start()

    def swapped_b():
        pltpu.make_async_copy(b_in, b.at[own_pair, half, own_lanes], local_sem.at[2]).wait()
        remote(b_in, b.at[own_pair, other, own_lanes], swap_send.at[2], swap_recv.at[2], partner).wait()

    def swapped_a(u):
        pltpu.make_async_copy(attn.at[u], a.at[u, :, half], local_sem.at[u]).wait()
        remote(attn.at[u], a.at[u, :, other], swap_send.at[u], swap_recv.at[u], partner).wait()

    def b_copy(hop, way, receive=False):
        origin = z - hop if way == 0 else z + hop
        if receive:
            origin = origin - 1 if way == 0 else origin + 1
        pair, lanes = b_cols(origin)
        rows = pl.ds(0, 1024) if hop < 3 else pl.ds(512 * way, 512)
        block = b.at[pair, rows, lanes]
        return remote(block, block, b_send.at[hop, way], b_recv.at[hop, way], zr if way == 0 else zl)

    a_moves = [(0, 2, 0), (1, 3, 1), (1, 4, 0), (0, 5, 1), (2, 6, 0), (3, 7, 1)]

    def a_copy(move):
        src, dst, way = a_moves[move]
        return remote(a.at[src], a.at[dst], a_send.at[move], a_recv.at[dst], xr if way == 0 else xl)

    def take_a(u):
        swapped_a(u)

        @pl.when(c == 1)
        def _():
            square = (128, 128)
            diagonal = lax.broadcasted_iota(jnp.int32, square, 0) == lax.broadcasted_iota(jnp.int32, square, 1)
            for h in range(2):
                keep = jnp.where(tokens[2 * u + h : 2 * u + h + 1, :] != 0, 1.0, 0.0).astype(F32)
                column = jnp.sum(jnp.where(diagonal, keep, 0.0), axis=1, keepdims=True).astype(BF16)
                a[u, 128 * h : 128 * h + 128, :] = a[u, 128 * h : 128 * h + 128, :] * column

    swapped_b()
    for way in range(2):
        b_copy(0, way).start()
    take_a(0)
    a_copy(0).start()
    take_a(1)
    a_copy(1).start()
    a_copy(2).start()
    a_copy(3).start()
    acc[...] = jnp.zeros_like(acc)
    for hop in range(4):
        for way in range(2):
            b_copy(hop, way, receive=True).wait_recv()
            if hop < 3:
                b_copy(hop + 1, way).start()
        if hop == 1:
            for move in range(2):
                a_copy(move).wait_recv()
                a_copy(move + 4).start()

    y_right, y_left, y_across = lax.rem(y + 1, 4), lax.rem(y + 3, 4), lax.rem(y + 2, 4)

    def relay_copy(k, way):
        return remote(s1.at[k, way], relay.at[k, way], s1_send.at[k, way], s1_recv.at[k, way], yr if way == 0 else yl)

    def fin_copy(k, way):
        return remote(s2.at[k, way], fin.at[k, way], s2_send.at[k, way], s2_recv.at[k, way], yr if way == 0 else yl)

    def r_copy(k, move):
        src, dst, way = [
            (rq.at[c, 0, k], rq.at[c, 3, k], 0),
            (rq.at[c, 0, k], rq.at[c, 1, k], 1),
            (rq.at[c, 3, k, pl.ds(0, 128)], rq.at[c, 2, k, pl.ds(0, 128)], 0),
            (rq.at[c, 1, k, pl.ds(128, 128)], rq.at[c, 2, k, pl.ds(128, 128)], 1),
        ][move]
        return remote(src, dst, r_send.at[k, move], r_recv.at[k, move], rr if way == 0 else rl)

    def q_copy(k, slot, receive=False):
        block = rq.at[1 - c if receive else c, slot, k]
        return remote(block, block, q_send.at[k, slot], q_recv.at[k, slot], partner)

    def q_copy_in(k, slot):
        block = rq.at[0, slot, k, pl.ds(128, 128)]
        return remote(block, block, q_send.at[k, slot], q_recv.at[k, slot], partner)

    def hand_over(k, slot, act):
        pl.when(c == 0)(lambda: getattr(q_copy_in(k, slot), act)())
        pl.when(c == 1)(lambda: getattr(q_copy(k, slot), act)())

    def tick(i, carry):
        def stage(lag, body):
            k = i - lag * LAG
            pl.when((k >= 0) & (k < 8))(functools.partial(body, k))

        def first(k):
            @pl.when(k >= 4)
            def _():
                remote(a.at[k], a.at[k], a_send.at[0], a_recv.at[k], xr).wait_recv()

            p = dot(a[k], b[y_across]).astype(BF16)
            s1[k, 0] = p[:128]
            s1[k, 1] = p[128:]
            for way in range(2):
                relay_copy(k, way).start()

        def second(k):
            for way, target in ((0, y_right), (1, y_left)):
                p = dot(a[k], b[target])
                relay_copy(k, way).wait_recv()
                if way == 0:
                    s2[k, 0, :128] = (p[:128] + relay[k, 0].astype(F32)).astype(BF16)
                    s2[k, 0, 128:] = p[128:].astype(BF16)
                else:
                    s2[k, 1, :128] = p[:128].astype(BF16)
                    s2[k, 1, 128:] = (p[128:] + relay[k, 1].astype(F32)).astype(BF16)
                fin_copy(k, way).start()

        def third(k):
            p = dot(a[k], b[y])
            for way in range(2):
                fin_copy(k, way).wait_recv()
            total = p + fin[k, 0].astype(F32) + fin[k, 1].astype(F32)

            @pl.when(c == 0)
            def _():
                rq[0, 0, k] = total.T.astype(BF16)

            @pl.when(c == 1)
            def _():
                rq[1, 0, k] = total.astype(BF16)

            r_copy(k, 0).start()
            r_copy(k, 1).start()
            hand_over(k, 0, "start")

        def fourth(k):
            for move, slot in ((0, 3), (1, 1)):
                r_copy(k, move).wait_recv()
                r_copy(k, move + 2).start()
                hand_over(k, slot, "start")

        def fifth(k):
            r_copy(k, 2).wait_recv()
            r_copy(k, 3).wait_recv()
            hand_over(k, 2, "start")

        stage(0, first)
        stage(1, second)
        stage(2, third)
        stage(3, fourth)
        stage(4, fifth)
        return carry

    lax.fori_loop(0, 8 + 4 * LAG, tick, 0)

    odd = lax.rem(z, 2)

    lanes = pl.ds(pl.multiple_of(c * 128, 128), 128)

    def product(pair):
        slot = lax.rem(pair - y + 4, 4)

        @pl.when(c == 0)
        def _():
            def take(k, carry):
                q_copy(k, slot, receive=True).wait_recv()
                return carry

            lax.fori_loop(0, 8, take, 0)

        for ds in range(4):
            for u in range(2):
                squares = 0.0
                for h in range(2):
                    rows = slice(128 * h, 128 * h + 128)
                    left = jnp.concatenate(
                        [rq[0, dx, STEP[(ds - dx) % 4, u], lanes, rows] for dx in range(4)], axis=0
                    )
                    coeff = dot(left, rq[1, slot, STEP[ds, u], rows, :])
                    squares = squares + coeff * coeff
                acc[pair] += squares

    def part(d, upper):
        zz = lax.rem(z + d + 16, 8)
        return acc[lax.div(zz, 2), 256 * upper : 256 * upper + 256, pl.ds(pl.multiple_of(lax.rem(zz, 2) * 128, 128), 128)]

    def o_copy(way, i):
        return remote(osend.at[way, i], orecv.at[way, i], o_send.at[way, i], o_recv.at[way, i], zr if way == 0 else zl)

    def pass_on(way, i):
        d = 4 - (i + 1) // 2
        block = part(d if way == 0 else -d, (i % 2) ^ way)
        if i >= 2:
            o_copy(way, i - 2).wait_recv()
            block = block + orecv[way, i - 2]
        osend[way, i] = block
        o_copy(way, i).start()

    even = odd == 0

    def passes(steps_even, steps_odd):
        for now, steps in ((even, steps_even), (jnp.logical_not(even), steps_odd)):

            @pl.when(now)
            def _(steps=steps):
                for way, i in steps:
                    pass_on(way, i)

    @pl.when(c == 1)
    def _():
        def take(k, carry):
            for slot in range(4):
                q_copy_in(k, slot).wait_recv()
            return carry

        lax.fori_loop(0, 8, take, 0)

    late = [(way, i) for i in range(3, 7) for way in range(2)]
    steps = [
        ([(0, 0), (1, 0), (1, 1)], [(0, 0), (1, 0), (0, 1)]),
        ([(0, 1), (0, 2), (1, 2)], [(1, 1), (0, 2), (1, 2)]),
    ]
    def squares_of(n, carry):
        offset = jnp.where(n == 0, 2, jnp.where(n == 1, 1 + 2 * odd, jnp.where(n == 2, 3 - 2 * odd, 0)))
        product(lax.rem(lax.div(z, 2) + offset, 4))
        for m in range(2):
            pl.when(n == m)(functools.partial(passes, *steps[m]))
        return carry

    lax.fori_loop(0, 4, squares_of, 0)
    for way, i in late:
        pass_on(way, i)

    for i in (5, 6):
        for way in range(2):
            o_copy(way, i).wait_recv()
    for upper in range(2):
        total = (part(0, upper) + orecv[0, 6 - upper] + orecv[1, 5 + upper]) * (1.0 / 128.0)
        for s in range(2):
            place = lax.rem(x + 2 * upper + s, 4)
            out[pl.ds(pl.multiple_of(place * 128, 128), 128), :] = total[128 * s : 128 * s + 128]

    for hop in range(4):
        for way in range(2):
            b_copy(hop, way).wait_send()
    for move in range(6):
        a_copy(move).wait_send()

    def sent(k, carry):
        for way in range(2):
            relay_copy(k, way).wait_send()
            fin_copy(k, way).wait_send()
        for move in range(4):
            r_copy(k, move).wait_send()
            hand_over(k, move, "wait_send")
        return carry

    lax.fori_loop(0, 8, sent, 0)
    for i in range(7):
        for way in range(2):
            o_copy(way, i).wait_send()


def on_device(token_ids, attn_out, cotangent, basis_in, basis_out):
    dma = pltpu.SemaphoreType.DMA
    return pl.pallas_call(
        kernel,
        out_shape=jax.ShapeDtypeStruct((512, 128), F32),
        in_specs=[pl.BlockSpec(memory_space=pltpu.VMEM)] + [pl.BlockSpec(memory_space=pl.ANY)] * 4,
        out_specs=pl.BlockSpec(memory_space=pltpu.VMEM),
        scratch_shapes=[
            pltpu.VMEM((8, 256, 1024), BF16),
            pltpu.VMEM((4, 1024, 256), BF16),
            pltpu.VMEM((8, 2, 128, 256), BF16),
            pltpu.VMEM((8, 2, 128, 256), BF16),
            pltpu.VMEM((8, 2, 256, 256), BF16),
            pltpu.VMEM((8, 2, 256, 256), BF16),
            pltpu.VMEM((2, 4, 8, 256, 256), BF16),
            pltpu.VMEM((4, 512, 256), F32),
            pltpu.VMEM((2, 7, 256, 128), F32),
            pltpu.VMEM((2, 7, 256, 128), F32),
            dma((3,)), dma((3,)), dma((3,)),
            dma((4, 2)), dma((4, 2)),
            dma((6,)), dma((8,)),
            dma((8, 2)), dma((8, 2)), dma((8, 2)), dma((8, 2)),
            dma((8, 4)), dma((8, 4)), dma((8, 4)), dma((8, 4)),
            dma((2, 7)), dma((2, 7)),
        ],
        compiler_params=pltpu.CompilerParams(
            collective_id=0, has_side_effects=True, vmem_limit_bytes=60 * 1024 * 1024
        ),
    )(token_ids, attn_out.reshape(2, 256, 512), cotangent.reshape(2, 256, 512), basis_in, basis_out)


def solution(mesh):
    return jax.shard_map(
        on_device,
        mesh=mesh,
        in_specs=(
            P("ex", None),
            P("ex", None, "tp"),
            P("ex", None, "tp"),
            P("tp", "ex"),
            P("tp", "ex"),
        ),
        out_specs=P("tp", "ex"),
        check_vma=False,
    )
```

```python
import functools

import jax
import jax.numpy as jnp
from jax import lax
from jax.experimental import pallas as pl
from jax.experimental.pallas import tpu as pltpu
from jax.sharding import PartitionSpec as P

MESH = pl.DeviceIdType.MESH
BF16 = jnp.bfloat16
F32 = jnp.float32
STEP = {(0, 0): 0, (0, 1): 1, (3, 0): 2, (1, 1): 3, (3, 1): 4, (1, 0): 5, (2, 0): 6, (2, 1): 7}
LAG = 2


def remote(src, dst, send, recv, device):
    return pltpu.make_async_remote_copy(
        src_ref=src, dst_ref=dst, send_sem=send, recv_sem=recv, device_id=device, device_id_type=MESH
    )


def dot(a, b):
    return jnp.dot(a, b, preferred_element_type=F32)


def kernel(
    tokens, attn, cot, b_in, b_out, out,
    a, b, s1, relay, s2, fin, rq, acc, osend, orecv,
    local_sem, swap_send, swap_recv, b_send, b_recv, a_send, a_recv,
    s1_send, s1_recv, s2_send, s2_recv, r_send, r_recv, q_send, q_recv, o_send, o_recv,
):
    t, e = lax.axis_index("tp"), lax.axis_index("ex")
    y, c = lax.div(t, 2), lax.rem(t, 2)
    z, x = lax.div(e, 4), lax.rem(e, 4)
    xr, xl = (t, z * 4 + lax.rem(x + 1, 4)), (t, z * 4 + lax.rem(x + 3, 4))
    yr, yl = (lax.rem(y + 1, 4) * 2 + c, e), (lax.rem(y + 3, 4) * 2 + c, e)
    zr, zl = (t, lax.rem(z + 1, 8) * 4 + x), (t, lax.rem(z + 7, 8) * 4 + x)
    partner = (y * 2 + 1 - c, e)
    rr = (xr[0] * (1 - c) + yr[0] * c, xr[1] * (1 - c) + yr[1] * c)
    rl = (xl[0] * (1 - c) + yl[0] * c, xl[1] * (1 - c) + yl[1] * c)

    barrier = pltpu.get_barrier_semaphore()
    for device in (xr, xl, yr, yl, zr, zl, partner):
        pl.semaphore_signal(barrier, inc=1, device_id=device, device_id_type=MESH)
    pl.semaphore_wait(barrier, 7)

    half = pl.ds(pl.multiple_of(c * 512, 512), 512)
    other = pl.ds(pl.multiple_of((1 - c) * 512, 512), 512)

    def b_cols(zz):
        zz = lax.rem(zz + 16, 8)
        return lax.div(zz, 2), pl.ds(pl.multiple_of(lax.rem(zz, 2) * 128, 128), 128)

    own_pair, own_lanes = b_cols(z)

    def swap(mine_a, mine_b, theirs_a, theirs_b):
        def copies():
            yield pltpu.make_async_copy(mine_b, b.at[own_pair, half, own_lanes], local_sem.at[2])
            yield remote(theirs_b, b.at[own_pair, half, own_lanes], swap_send.at[2], swap_recv.at[2], partner)
            for u in range(2):
                yield pltpu.make_async_copy(mine_a.at[u], a.at[u, :, half], local_sem.at[u])
                yield remote(theirs_a.at[u], a.at[u, :, half], swap_send.at[u], swap_recv.at[u], partner)

        return copies

    @pl.when(c == 0)
    def _():
        for copy in swap(attn, b_in, cot, b_out)():
            copy.start()

    @pl.when(c == 1)
    def _():
        for copy in swap(cot, b_out, attn, b_in)():
            copy.start()

    def local_b():
        pltpu.make_async_copy(b_in, b.at[own_pair, half, own_lanes], local_sem.at[2]).wait()

    def swapped_b():
        remote(b_in, b.at[own_pair, other, own_lanes], swap_send.at[2], swap_recv.at[2], partner).wait()

    def swapped_a(u):
        pltpu.make_async_copy(attn.at[u], a.at[u, :, half], local_sem.at[u]).wait()
        remote(attn.at[u], a.at[u, :, other], swap_send.at[u], swap_recv.at[u], partner).wait()

    def b_copy(hop, way, j, receive=False):
        origin = z - hop if way == 0 else z + hop
        if receive:
            origin = origin - 1 if way == 0 else origin + 1
        pair, lanes = b_cols(origin)
        block = b.at[pair, other if j else half, lanes]
        return remote(block, block, b_send.at[hop, way, j], b_recv.at[hop, way, j], zr if way == 0 else zl)

    a_moves = [(0, 2, 0), (1, 3, 1), (1, 4, 0), (0, 5, 1), (2, 6, 0), (3, 7, 1)]

    def a_copy(move):
        src, dst, way = a_moves[move]
        return remote(a.at[src], a.at[dst], a_send.at[move], a_recv.at[dst], xr if way == 0 else xl)

    def take_a(u):
        swapped_a(u)

        @pl.when(c == 1)
        def _():
            square = (128, 128)
            diagonal = lax.broadcasted_iota(jnp.int32, square, 0) == lax.broadcasted_iota(jnp.int32, square, 1)
            for h in range(2):
                keep = jnp.where(tokens[2 * u + h : 2 * u + h + 1, :] != 0, 1.0, 0.0).astype(F32)
                column = jnp.sum(jnp.where(diagonal, keep, 0.0), axis=1, keepdims=True).astype(BF16)
                a[u, 128 * h : 128 * h + 128, :] = a[u, 128 * h : 128 * h + 128, :] * column

    local_b()
    for way in range(2):
        b_copy(0, way, 0).start()
    swapped_b()
    for way in range(2):
        b_copy(0, way, 1).start()
    take_a(0)
    a_copy(0).start()
    take_a(1)
    a_copy(1).start()
    a_copy(2).start()
    a_copy(3).start()
    acc[...] = jnp.zeros_like(acc)
    for hop in range(4):
        for j in range(2):
            for way in range(2):
                if hop < 3 or j == way:
                    b_copy(hop, way, j, receive=True).wait_recv()
                if hop < 2 or (hop == 2 and j == way):
                    b_copy(hop + 1, way, j).start()
        if hop == 1:
            for move in range(2):
                a_copy(move).wait_recv()
                a_copy(move + 4).start()

    y_right, y_left, y_across = lax.rem(y + 1, 4), lax.rem(y + 3, 4), lax.rem(y + 2, 4)

    def relay_copy(k, way):
        return remote(s1.at[k, way], relay.at[k, way], s1_send.at[k, way], s1_recv.at[k, way], yr if way == 0 else yl)

    def fin_copy(k, way):
        return remote(s2.at[k, way], fin.at[k, way], s2_send.at[k, way], s2_recv.at[k, way], yr if way == 0 else yl)

    def r_copy(k, move):
        src, dst, way = [
            (rq.at[c, 0, k], rq.at[c, 3, k], 0),
            (rq.at[c, 0, k], rq.at[c, 1, k], 1),
            (rq.at[c, 3, k, pl.ds(0, 128)], rq.at[c, 2, k, pl.ds(0, 128)], 0),
            (rq.at[c, 1, k, pl.ds(128, 128)], rq.at[c, 2, k, pl.ds(128, 128)], 1),
        ][move]
        return remote(src, dst, r_send.at[k, move], r_recv.at[k, move], rr if way == 0 else rl)

    def q_copy(k, slot, receive=False):
        block = rq.at[1 - c if receive else c, slot, k]
        return remote(block, block, q_send.at[k, slot], q_recv.at[k, slot], partner)

    def q_copy_in(k, slot):
        block = rq.at[0, slot, k, pl.ds(128, 128)]
        return remote(block, block, q_send.at[k, slot], q_recv.at[k, slot], partner)

    def hand_over(k, slot, act):
        pl.when(c == 0)(lambda: getattr(q_copy_in(k, slot), act)())
        pl.when(c == 1)(lambda: getattr(q_copy(k, slot), act)())

    def tick(i, carry):
        def stage(lag, body):
            k = i - lag * LAG
            pl.when((k >= 0) & (k < 8))(functools.partial(body, k))

        def first(k):
            @pl.when(k >= 4)
            def _():
                remote(a.at[k], a.at[k], a_send.at[0], a_recv.at[k], xr).wait_recv()

            p = dot(a[k], b[y_across]).astype(BF16)
            s1[k, 0] = p[:128]
            s1[k, 1] = p[128:]
            for way in range(2):
                relay_copy(k, way).start()

        def second(k):
            for way, target in ((0, y_right), (1, y_left)):
                p = dot(a[k], b[target])
                relay_copy(k, way).wait_recv()
                if way == 0:
                    s2[k, 0, :128] = (p[:128] + relay[k, 0].astype(F32)).astype(BF16)
                    s2[k, 0, 128:] = p[128:].astype(BF16)
                else:
                    s2[k, 1, :128] = p[:128].astype(BF16)
                    s2[k, 1, 128:] = (p[128:] + relay[k, 1].astype(F32)).astype(BF16)
                fin_copy(k, way).start()

        def third(k):
            p = dot(a[k], b[y])
            for way in range(2):
                fin_copy(k, way).wait_recv()
            total = p + fin[k, 0].astype(F32) + fin[k, 1].astype(F32)

            @pl.when(c == 0)
            def _():
                rq[0, 0, k] = total.T.astype(BF16)

            @pl.when(c == 1)
            def _():
                rq[1, 0, k] = total.astype(BF16)

            r_copy(k, 0).start()
            r_copy(k, 1).start()
            hand_over(k, 0, "start")

        def fourth(k):
            for move, slot in ((0, 3), (1, 1)):
                r_copy(k, move).wait_recv()
                r_copy(k, move + 2).start()
                hand_over(k, slot, "start")

        def fifth(k):
            r_copy(k, 2).wait_recv()
            r_copy(k, 3).wait_recv()
            hand_over(k, 2, "start")

        stage(0, first)
        stage(1, second)
        stage(2, third)
        stage(3, fourth)
        stage(4, fifth)
        return carry

    lax.fori_loop(0, 8 + 4 * LAG, tick, 0)

    odd = lax.rem(z, 2)

    lanes = pl.ds(pl.multiple_of(c * 128, 128), 128)

    def product(pair):
        slot = lax.rem(pair - y + 4, 4)

        @pl.when(c == 0)
        def _():
            def take(k, carry):
                q_copy(k, slot, receive=True).wait_recv()
                return carry

            lax.fori_loop(0, 8, take, 0)

        for ds in range(4):
            for u in range(2):
                squares = 0.0
                for h in range(2):
                    rows = slice(128 * h, 128 * h + 128)
                    left = jnp.concatenate(
                        [rq[0, dx, STEP[(ds - dx) % 4, u], lanes, rows] for dx in range(4)], axis=0
                    )
                    coeff = dot(left, rq[1, slot, STEP[ds, u], rows, :])
                    squares = squares + coeff * coeff
                acc[pair] += squares

    def part(d, upper):
        zz = lax.rem(z + d + 16, 8)
        return acc[lax.div(zz, 2), 256 * upper : 256 * upper + 256, pl.ds(pl.multiple_of(lax.rem(zz, 2) * 128, 128), 128)]

    def o_copy(way, i):
        return remote(osend.at[way, i], orecv.at[way, i], o_send.at[way, i], o_recv.at[way, i], zr if way == 0 else zl)

    def pass_on(way, i):
        d = 4 - (i + 1) // 2
        block = part(d if way == 0 else -d, (i % 2) ^ way)
        if i >= 2:
            o_copy(way, i - 2).wait_recv()
            block = block + orecv[way, i - 2]
        osend[way, i] = block
        o_copy(way, i).start()

    even = odd == 0

    def passes(steps_even, steps_odd):
        for now, steps in ((even, steps_even), (jnp.logical_not(even), steps_odd)):

            @pl.when(now)
            def _(steps=steps):
                for way, i in steps:
                    pass_on(way, i)

    @pl.when(c == 1)
    def _():
        def take(k, carry):
            for slot in range(4):
                q_copy_in(k, slot).wait_recv()
            return carry

        lax.fori_loop(0, 8, take, 0)

    late = [(way, i) for i in range(3, 7) for way in range(2)]
    steps = [
        ([(0, 0), (1, 0), (1, 1)], [(0, 0), (1, 0), (0, 1)]),
        ([(0, 1), (0, 2), (1, 2)], [(1, 1), (0, 2), (1, 2)]),
    ]
    def squares_of(n, carry):
        offset = jnp.where(n == 0, 2, jnp.where(n == 1, 1 + 2 * odd, jnp.where(n == 2, 3 - 2 * odd, 0)))
        product(lax.rem(lax.div(z, 2) + offset, 4))
        for m in range(2):
            pl.when(n == m)(functools.partial(passes, *steps[m]))
        return carry

    lax.fori_loop(0, 4, squares_of, 0)
    for way, i in late:
        pass_on(way, i)

    for i in (5, 6):
        for way in range(2):
            o_copy(way, i).wait_recv()
    for upper in range(2):
        total = (part(0, upper) + orecv[0, 6 - upper] + orecv[1, 5 + upper]) * (1.0 / 128.0)
        for s in range(2):
            place = lax.rem(x + 2 * upper + s, 4)
            out[pl.ds(pl.multiple_of(place * 128, 128), 128), :] = total[128 * s : 128 * s + 128]

    for hop in range(4):
        for way in range(2):
            for j in range(2):
                if hop < 3 or j == way:
                    b_copy(hop, way, j).wait_send()
    for move in range(6):
        a_copy(move).wait_send()

    def sent(k, carry):
        for way in range(2):
            relay_copy(k, way).wait_send()
            fin_copy(k, way).wait_send()
        for move in range(4):
            r_copy(k, move).wait_send()
            hand_over(k, move, "wait_send")
        return carry

    lax.fori_loop(0, 8, sent, 0)
    for i in range(7):
        for way in range(2):
            o_copy(way, i).wait_send()


def on_device(token_ids, attn_out, cotangent, basis_in, basis_out):
    dma = pltpu.SemaphoreType.DMA
    return pl.pallas_call(
        kernel,
        out_shape=jax.ShapeDtypeStruct((512, 128), F32),
        in_specs=[pl.BlockSpec(memory_space=pltpu.VMEM)] + [pl.BlockSpec(memory_space=pl.ANY)] * 4,
        out_specs=pl.BlockSpec(memory_space=pltpu.VMEM),
        scratch_shapes=[
            pltpu.VMEM((8, 256, 1024), BF16),
            pltpu.VMEM((4, 1024, 256), BF16),
            pltpu.VMEM((8, 2, 128, 256), BF16),
            pltpu.VMEM((8, 2, 128, 256), BF16),
            pltpu.VMEM((8, 2, 256, 256), BF16),
            pltpu.VMEM((8, 2, 256, 256), BF16),
            pltpu.VMEM((2, 4, 8, 256, 256), BF16),
            pltpu.VMEM((4, 512, 256), F32),
            pltpu.VMEM((2, 7, 256, 128), F32),
            pltpu.VMEM((2, 7, 256, 128), F32),
            dma((3,)), dma((3,)), dma((3,)),
            dma((4, 2, 2)), dma((4, 2, 2)),
            dma((6,)), dma((8,)),
            dma((8, 2)), dma((8, 2)), dma((8, 2)), dma((8, 2)),
            dma((8, 4)), dma((8, 4)), dma((8, 4)), dma((8, 4)),
            dma((2, 7)), dma((2, 7)),
        ],
        compiler_params=pltpu.CompilerParams(
            collective_id=0, has_side_effects=True, vmem_limit_bytes=60 * 1024 * 1024
        ),
    )(token_ids, attn_out.reshape(2, 256, 512), cotangent.reshape(2, 256, 512), basis_in, basis_out)


def solution(mesh):
    return jax.shard_map(
        on_device,
        mesh=mesh,
        in_specs=(
            P("ex", None),
            P("ex", None, "tp"),
            P("ex", None, "tp"),
            P("tp", "ex"),
            P("tp", "ex"),
        ),
        out_specs=P("tp", "ex"),
        check_vma=False,
    )
```

```python
import functools

import jax
import jax.numpy as jnp
from jax import lax
from jax.experimental import pallas as pl
from jax.experimental.pallas import tpu as pltpu
from jax.sharding import PartitionSpec as P

MESH = pl.DeviceIdType.MESH
BF16 = jnp.bfloat16
F32 = jnp.float32
STEP = {(0, 0): 0, (0, 1): 1, (3, 0): 2, (1, 1): 3, (3, 1): 4, (1, 0): 5, (2, 0): 6, (2, 1): 7}
LAG = 2


def remote(src, dst, send, recv, device):
    return pltpu.make_async_remote_copy(
        src_ref=src, dst_ref=dst, send_sem=send, recv_sem=recv, device_id=device, device_id_type=MESH
    )


def dot(a, b):
    return jnp.dot(a, b, preferred_element_type=F32)


def kernel(
    tokens, attn, cot, b_in, b_out, out,
    a, b, s1, relay, s2, fin, rq, acc, osend, orecv,
    local_sem, swap_send, swap_recv, b_send, b_recv, a_send, a_recv,
    s1_send, s1_recv, s2_send, s2_recv, r_send, r_recv, q_send, q_recv, o_send, o_recv,
):
    t, e = lax.axis_index("tp"), lax.axis_index("ex")
    y, c = lax.div(t, 2), lax.rem(t, 2)
    z, x = lax.div(e, 4), lax.rem(e, 4)
    xr, xl = (t, z * 4 + lax.rem(x + 1, 4)), (t, z * 4 + lax.rem(x + 3, 4))
    yr, yl = (lax.rem(y + 1, 4) * 2 + c, e), (lax.rem(y + 3, 4) * 2 + c, e)
    zr, zl = (t, lax.rem(z + 1, 8) * 4 + x), (t, lax.rem(z + 7, 8) * 4 + x)
    partner = (y * 2 + 1 - c, e)
    rr = (xr[0] * (1 - c) + yr[0] * c, xr[1] * (1 - c) + yr[1] * c)
    rl = (xl[0] * (1 - c) + yl[0] * c, xl[1] * (1 - c) + yl[1] * c)

    barrier = pltpu.get_barrier_semaphore()
    for device in (xr, xl, yr, yl, zr, zl, partner):
        pl.semaphore_signal(barrier, inc=1, device_id=device, device_id_type=MESH)
    pl.semaphore_wait(barrier, 7)

    half = pl.ds(pl.multiple_of(c * 512, 512), 512)
    other = pl.ds(pl.multiple_of((1 - c) * 512, 512), 512)

    def b_cols(zz):
        zz = lax.rem(zz + 16, 8)
        return lax.div(zz, 2), pl.ds(pl.multiple_of(lax.rem(zz, 2) * 128, 128), 128)

    own_pair, own_lanes = b_cols(z)

    def swap(mine_a, mine_b, theirs_a, theirs_b):
        def copies():
            yield pltpu.make_async_copy(mine_b, b.at[own_pair, half, own_lanes], local_sem.at[2])
            yield remote(theirs_b, b.at[own_pair, half, own_lanes], swap_send.at[2], swap_recv.at[2], partner)
            for u in range(2):
                yield pltpu.make_async_copy(mine_a.at[u], a.at[u, :, half], local_sem.at[u])
                yield remote(theirs_a.at[u], a.at[u, :, half], swap_send.at[u], swap_recv.at[u], partner)

        return copies

    @pl.when(c == 0)
    def _():
        for copy in swap(attn, b_in, cot, b_out)():
            copy.start()

    @pl.when(c == 1)
    def _():
        for copy in swap(cot, b_out, attn, b_in)():
            copy.start()

    def local_b():
        pltpu.make_async_copy(b_in, b.at[own_pair, half, own_lanes], local_sem.at[2]).wait()

    def swapped_b():
        remote(b_in, b.at[own_pair, other, own_lanes], swap_send.at[2], swap_recv.at[2], partner).wait()

    def swapped_a(u):
        pltpu.make_async_copy(attn.at[u], a.at[u, :, half], local_sem.at[u]).wait()
        remote(attn.at[u], a.at[u, :, other], swap_send.at[u], swap_recv.at[u], partner).wait()

    def b_copy(hop, way, j, receive=False):
        origin = z - hop if way == 0 else z + hop
        if receive:
            origin = origin - 1 if way == 0 else origin + 1
        pair, lanes = b_cols(origin)
        block = b.at[pair, other if j else half, lanes]
        return remote(block, block, b_send.at[hop, way, j], b_recv.at[hop, way, j], zr if way == 0 else zl)

    a_moves = [(0, 2, 0), (1, 3, 1), (1, 4, 0), (0, 5, 1), (2, 6, 0), (3, 7, 1)]

    def a_copy(move):
        src, dst, way = a_moves[move]
        return remote(a.at[src], a.at[dst], a_send.at[move], a_recv.at[dst], xr if way == 0 else xl)

    def take_a(u):
        swapped_a(u)

        @pl.when(c == 1)
        def _():
            square = (128, 128)
            diagonal = lax.broadcasted_iota(jnp.int32, square, 0) == lax.broadcasted_iota(jnp.int32, square, 1)
            for h in range(2):
                keep = jnp.where(tokens[2 * u + h : 2 * u + h + 1, :] != 0, 1.0, 0.0).astype(F32)
                column = jnp.sum(jnp.where(diagonal, keep, 0.0), axis=1, keepdims=True).astype(BF16)
                a[u, 128 * h : 128 * h + 128, :] = a[u, 128 * h : 128 * h + 128, :] * column

    local_b()
    for way in range(2):
        b_copy(0, way, 0).start()
    swapped_b()
    for way in range(2):
        b_copy(0, way, 1).start()
    take_a(0)
    a_copy(0).start()
    take_a(1)
    a_copy(1).start()
    a_copy(2).start()
    a_copy(3).start()
    acc[...] = jnp.zeros_like(acc)
    for hop in range(4):
        for j in range(2):
            for way in range(2):
                if hop < 3 or j == way:
                    b_copy(hop, way, j, receive=True).wait_recv()
                if hop < 2 or (hop == 2 and j == way):
                    b_copy(hop + 1, way, j).start()
        if hop == 2:
            for move in range(2):
                a_copy(move).wait_recv()
                a_copy(move + 4).start()

    y_right, y_left, y_across = lax.rem(y + 1, 4), lax.rem(y + 3, 4), lax.rem(y + 2, 4)

    def relay_copy(k, way):
        return remote(s1.at[k, way], relay.at[k, way], s1_send.at[k, way], s1_recv.at[k, way], yr if way == 0 else yl)

    def fin_copy(k, way):
        return remote(s2.at[k, way], fin.at[k, way], s2_send.at[k, way], s2_recv.at[k, way], yr if way == 0 else yl)

    def r_copy(k, move):
        src, dst, way = [
            (rq.at[c, 0, k], rq.at[c, 3, k], 0),
            (rq.at[c, 0, k], rq.at[c, 1, k], 1),
            (rq.at[c, 3, k, pl.ds(0, 128)], rq.at[c, 2, k, pl.ds(0, 128)], 0),
            (rq.at[c, 1, k, pl.ds(128, 128)], rq.at[c, 2, k, pl.ds(128, 128)], 1),
        ][move]
        return remote(src, dst, r_send.at[k, move], r_recv.at[k, move], rr if way == 0 else rl)

    def q_copy(k, slot, receive=False):
        block = rq.at[1 - c if receive else c, slot, k]
        return remote(block, block, q_send.at[k, slot], q_recv.at[k, slot], partner)

    def q_copy_in(k, slot):
        block = rq.at[0, slot, k, pl.ds(128, 128)]
        return remote(block, block, q_send.at[k, slot], q_recv.at[k, slot], partner)

    def hand_over(k, slot, act):
        pl.when(c == 0)(lambda: getattr(q_copy_in(k, slot), act)())
        pl.when(c == 1)(lambda: getattr(q_copy(k, slot), act)())

    def tick(i, carry):
        def stage(lag, body):
            k = i - lag * LAG
            pl.when((k >= 0) & (k < 8))(functools.partial(body, k))

        def first(k):
            @pl.when(k >= 4)
            def _():
                remote(a.at[k], a.at[k], a_send.at[0], a_recv.at[k], xr).wait_recv()

            p = dot(a[k], b[y_across]).astype(BF16)
            s1[k, 0] = p[:128]
            s1[k, 1] = p[128:]
            for way in range(2):
                relay_copy(k, way).start()

        def second(k):
            for way, target in ((0, y_right), (1, y_left)):
                p = dot(a[k], b[target])
                relay_copy(k, way).wait_recv()
                if way == 0:
                    s2[k, 0, :128] = (p[:128] + relay[k, 0].astype(F32)).astype(BF16)
                    s2[k, 0, 128:] = p[128:].astype(BF16)
                else:
                    s2[k, 1, :128] = p[:128].astype(BF16)
                    s2[k, 1, 128:] = (p[128:] + relay[k, 1].astype(F32)).astype(BF16)
                fin_copy(k, way).start()

        def third(k):
            p = dot(a[k], b[y])
            for way in range(2):
                fin_copy(k, way).wait_recv()
            total = p + fin[k, 0].astype(F32) + fin[k, 1].astype(F32)

            @pl.when(c == 0)
            def _():
                rq[0, 0, k] = total.T.astype(BF16)

            @pl.when(c == 1)
            def _():
                rq[1, 0, k] = total.astype(BF16)

            r_copy(k, 0).start()
            r_copy(k, 1).start()
            hand_over(k, 0, "start")

        def fourth(k):
            for move, slot in ((0, 3), (1, 1)):
                r_copy(k, move).wait_recv()
                r_copy(k, move + 2).start()
                hand_over(k, slot, "start")

        def fifth(k):
            r_copy(k, 2).wait_recv()
            r_copy(k, 3).wait_recv()
            hand_over(k, 2, "start")

        stage(0, first)
        stage(1, second)
        stage(2, third)
        stage(3, fourth)
        stage(4, fifth)
        return carry

    lax.fori_loop(0, 8 + 4 * LAG, tick, 0)

    odd = lax.rem(z, 2)

    lanes = pl.ds(pl.multiple_of(c * 128, 128), 128)

    def product(pair):
        slot = lax.rem(pair - y + 4, 4)

        @pl.when(c == 0)
        def _():
            def take(k, carry):
                q_copy(k, slot, receive=True).wait_recv()
                return carry

            lax.fori_loop(0, 8, take, 0)

        for ds in range(4):
            for u in range(2):
                squares = 0.0
                for h in range(2):
                    rows = slice(128 * h, 128 * h + 128)
                    left = jnp.concatenate(
                        [rq[0, dx, STEP[(ds - dx) % 4, u], lanes, rows] for dx in range(4)], axis=0
                    )
                    coeff = dot(left, rq[1, slot, STEP[ds, u], rows, :])
                    squares = squares + coeff * coeff
                acc[pair] += squares

    def part(d, upper):
        zz = lax.rem(z + d + 16, 8)
        return acc[lax.div(zz, 2), 256 * upper : 256 * upper + 256, pl.ds(pl.multiple_of(lax.rem(zz, 2) * 128, 128), 128)]

    def o_copy(way, i):
        return remote(osend.at[way, i], orecv.at[way, i], o_send.at[way, i], o_recv.at[way, i], zr if way == 0 else zl)

    def pass_on(way, i):
        d = 4 - (i + 1) // 2
        block = part(d if way == 0 else -d, (i % 2) ^ way)
        if i >= 2:
            o_copy(way, i - 2).wait_recv()
            block = block + orecv[way, i - 2]
        osend[way, i] = block
        o_copy(way, i).start()

    even = odd == 0

    def passes(steps_even, steps_odd):
        for now, steps in ((even, steps_even), (jnp.logical_not(even), steps_odd)):

            @pl.when(now)
            def _(steps=steps):
                for way, i in steps:
                    pass_on(way, i)

    @pl.when(c == 1)
    def _():
        def take(k, carry):
            for slot in range(4):
                q_copy_in(k, slot).wait_recv()
            return carry

        lax.fori_loop(0, 8, take, 0)

    late = [(way, i) for i in range(3, 7) for way in range(2)]
    steps = [
        ([(0, 0), (1, 0), (1, 1)], [(0, 0), (1, 0), (0, 1)]),
        ([(0, 1), (0, 2), (1, 2)], [(1, 1), (0, 2), (1, 2)]),
    ]
    def squares_of(n, carry):
        offset = jnp.where(n == 0, 2, jnp.where(n == 1, 1 + 2 * odd, jnp.where(n == 2, 3 - 2 * odd, 0)))
        product(lax.rem(lax.div(z, 2) + offset, 4))
        for m in range(2):
            pl.when(n == m)(functools.partial(passes, *steps[m]))
        return carry

    lax.fori_loop(0, 4, squares_of, 0)
    for way, i in late:
        pass_on(way, i)

    for i in (5, 6):
        for way in range(2):
            o_copy(way, i).wait_recv()
    for upper in range(2):
        total = (part(0, upper) + orecv[0, 6 - upper] + orecv[1, 5 + upper]) * (1.0 / 128.0)
        for s in range(2):
            place = lax.rem(x + 2 * upper + s, 4)
            out[pl.ds(pl.multiple_of(place * 128, 128), 128), :] = total[128 * s : 128 * s + 128]

    for hop in range(4):
        for way in range(2):
            for j in range(2):
                if hop < 3 or j == way:
                    b_copy(hop, way, j).wait_send()
    for move in range(6):
        a_copy(move).wait_send()

    def sent(k, carry):
        for way in range(2):
            relay_copy(k, way).wait_send()
            fin_copy(k, way).wait_send()
        for move in range(4):
            r_copy(k, move).wait_send()
            hand_over(k, move, "wait_send")
        return carry

    lax.fori_loop(0, 8, sent, 0)
    for i in range(7):
        for way in range(2):
            o_copy(way, i).wait_send()


def on_device(token_ids, attn_out, cotangent, basis_in, basis_out):
    dma = pltpu.SemaphoreType.DMA
    return pl.pallas_call(
        kernel,
        out_shape=jax.ShapeDtypeStruct((512, 128), F32),
        in_specs=[pl.BlockSpec(memory_space=pltpu.VMEM)] + [pl.BlockSpec(memory_space=pl.ANY)] * 4,
        out_specs=pl.BlockSpec(memory_space=pltpu.VMEM),
        scratch_shapes=[
            pltpu.VMEM((8, 256, 1024), BF16),
            pltpu.VMEM((4, 1024, 256), BF16),
            pltpu.VMEM((8, 2, 128, 256), BF16),
            pltpu.VMEM((8, 2, 128, 256), BF16),
            pltpu.VMEM((8, 2, 256, 256), BF16),
            pltpu.VMEM((8, 2, 256, 256), BF16),
            pltpu.VMEM((2, 4, 8, 256, 256), BF16),
            pltpu.VMEM((4, 512, 256), F32),
            pltpu.VMEM((2, 7, 256, 128), F32),
            pltpu.VMEM((2, 7, 256, 128), F32),
            dma((3,)), dma((3,)), dma((3,)),
            dma((4, 2, 2)), dma((4, 2, 2)),
            dma((6,)), dma((8,)),
            dma((8, 2)), dma((8, 2)), dma((8, 2)), dma((8, 2)),
            dma((8, 4)), dma((8, 4)), dma((8, 4)), dma((8, 4)),
            dma((2, 7)), dma((2, 7)),
        ],
        compiler_params=pltpu.CompilerParams(
            collective_id=0, has_side_effects=True, vmem_limit_bytes=60 * 1024 * 1024
        ),
    )(token_ids, attn_out.reshape(2, 256, 512), cotangent.reshape(2, 256, 512), basis_in, basis_out)


def solution(mesh):
    return jax.shard_map(
        on_device,
        mesh=mesh,
        in_specs=(
            P("ex", None),
            P("ex", None, "tp"),
            P("ex", None, "tp"),
            P("tp", "ex"),
            P("tp", "ex"),
        ),
        out_specs=P("tp", "ex"),
        check_vma=False,
    )
```
